32 devices in a mesh: dp: 8 (over z, y), mp: 4 (over x, core).
Axes of the slice: x: 2, y: 2, z: 4, core: 2. Of those that a mesh axis runs over, the one named last changes fastest.
Arguments:
- patches: bfloat16 [1152, 1024], P('mp', 'dp'), may hold values from -40 to 40
- counts: int32 [64], replicated, may hold values from 4 to 16, as said below
- dest: int32 [64], replicated, may hold values from 0 to 7, as said below
- w_qkv: bfloat16 [3, 1152, 1152], P(None, 'mp'), may hold values from -4 to 4
- w_out: bfloat16 [1152, 1152], P('mp'), may hold values from -0.1875 to 0.1875
- text: bfloat16 [64, 1152], P(('dp', 'mp')), may hold values from -6 to 6
Outputs:
- grad_image: float32 [64, 1152], P('dp', 'mp')
- grad_text: float32 [64, 1152], P(('dp', 'mp'))
The draws below stay inside these ranges and needn't reach their ends.
Inputs may be any that keep to these rules, and one draw needn't show every extreme that they name: `counts`: every dp index holds 8 images; on some dp index every image that is sent to it has 16 patches. `dest`: entries s * 8 to s * 8 + 7 are a permutation of 0 to 7: every dp index sends exactly one image to every dp index.
All inputs are finite; a program needn't handle non-finite values.
Results may differ from the reference program's by a relative error of at most 0.0046.
Values may be sent and summed in bfloat16 or wider, within the bound.
No kernel may reach another device: no remote copies, remote signals or barrier semaphores. Data moves between devices by JAX's collectives and lax.ppermute only.
A program may use at most 64 MiB of HBM per device.

```python
import math
import jax
import jax.numpy as jnp
from jax import lax

D = 1152
HEADS = 16
HD = 72
MAXP = 16
MINP = 4
IMG_DEV = 8
ROWS_DEV = 128
TOTAL = 64


def routing_plan(key):
    key_perm, key_count, key_full = jax.random.split(key, 3)
    perm_keys = jax.random.split(key_perm, IMG_DEV)
    dest_table = jax.vmap(lambda one_key: jax.random.permutation(one_key, IMG_DEV))(perm_keys).astype(jnp.int32)
    count_table = jax.random.randint(key_count, (IMG_DEV, IMG_DEV), MINP, MAXP + 1).astype(jnp.int32)
    full_target = jax.random.randint(key_full, (), 0, IMG_DEV).astype(jnp.int32)
    count_table = jnp.where(dest_table == full_target, MAXP, count_table).astype(jnp.int32)
    return (count_table.reshape(TOTAL), dest_table.reshape(TOTAL))


def draw_counts(key, part):
    return routing_plan(key)[0]


def draw_dest(key, part):
    return routing_plan(key)[1]


def draw_patches(key, part):
    key = jax.random.fold_in(key, 7)
    key_base, key_rows, key_cols = jax.random.split(key, 3)
    shape_all = (D, IMG_DEV * ROWS_DEV)
    column_scale = jnp.exp(jax.random.uniform(key_cols, (D, 1), jnp.float32, jnp.log(0.5), jnp.log(3.0)))
    row_scale = jnp.exp(jax.random.uniform(key_rows, (1, IMG_DEV * ROWS_DEV), jnp.float32, jnp.log(0.5), jnp.log(3.0)))
    values = jnp.clip(jax.random.normal(key_base, shape_all, jnp.float32), -4.0, 4.0) * row_scale * column_scale
    return values.astype(jnp.bfloat16)


def draw_w_qkv(key, part):
    key = jax.random.fold_in(key, 5)
    key_query, key_second, key_value = jax.random.split(key, 3)
    spread = D ** (-0.5)
    query_w = jnp.clip(jax.random.normal(key_query, (D, D), jnp.float32), -4.0, 4.0) * spread
    second = jnp.clip(jax.random.normal(key_second, (D, D), jnp.float32), -4.0, 4.0) * spread
    value_w = jnp.clip(jax.random.normal(key_value, (D, D), jnp.float32), -4.0, 4.0) * spread
    key_w = second
    stacked = jnp.clip(jnp.stack([query_w, key_w, value_w]), -4.0, 4.0)
    return jnp.transpose(stacked, (0, 2, 1)).astype(jnp.bfloat16)


def levels(rng, extent, cuts, least, high):
    def one(dim, shards_of):
        heights = jax.random.uniform(jax.random.fold_in(jax.random.fold_in(rng, 6), dim), (shards_of,), jnp.float32, least / len(cuts), high / len(cuts))
        return jnp.repeat(jnp.exp(heights), extent[dim] // shards_of).reshape((-1,) + (1,) * (len(extent) - dim - 1))

    loudness = one(*cuts[0])
    for cut in cuts[1:]:
        loudness = loudness * one(*cut)
    return loudness


def gaussian(stream_key, shape, scale, bound, pieces=(), kind=jnp.bfloat16):
    gain = levels(stream_key, shape, pieces, -0.22, 0.18) if pieces else 1.0
    entries = jax.random.normal(stream_key, shape, jnp.float32) * scale * gain
    return jnp.minimum(jnp.maximum(entries, -bound), bound).astype(kind)


def setup_inputs(seed: int = 0) -> dict:
    streams_of = jax.random.split(jax.random.key(seed), 7)
    return {
        "patches": draw_patches(jax.random.fold_in(streams_of[6], 71), 0),
        "counts": draw_counts(jax.random.fold_in(streams_of[6], 71), 0),
        "dest": draw_dest(jax.random.fold_in(streams_of[6], 71), 0),
        "w_qkv": draw_w_qkv(jax.random.fold_in(streams_of[6], 71), 0),
        "w_out": gaussian(streams_of[4], (D, D), D ** -0.5, 0.1875, ((0, 4),)),
        "text": gaussian(streams_of[5], (TOTAL, D), 1.0, 6.0, ((0, 32),)),
    }


def routing(counts, dest):
    count_table = counts.reshape(IMG_DEV, IMG_DEV)
    dest_table = dest.reshape(IMG_DEV, IMG_DEV)
    start_table = (jnp.cumsum(count_table, axis=1) - count_table).astype(jnp.int32)
    targets = jnp.arange(IMG_DEV, dtype=jnp.int32)
    chosen = dest_table[None, :, :] == targets[:, None, None]
    got_count = lax.optimization_barrier(jnp.sum(jnp.where(chosen, count_table[None], 0), axis=2)).astype(jnp.int32)
    got_start = lax.optimization_barrier(jnp.sum(jnp.where(chosen, start_table[None], 0), axis=2)).astype(jnp.int32)
    got_index = lax.optimization_barrier(jnp.sum(jnp.where(chosen, targets[None, None, :], 0), axis=2)).astype(jnp.int32)
    image_ids = (targets[None, :] * IMG_DEV + got_index).astype(jnp.int32)
    return (got_count, got_start, image_ids)

def reference(patches, counts, dest, w_qkv, w_out, text):
    got_count, got_start, image_ids = routing(counts, dest)
    source_rows = patches.T.reshape(IMG_DEV, ROWS_DEV, D)
    position = jnp.arange(MAXP, dtype=jnp.int32)
    sources = jnp.arange(IMG_DEV, dtype=jnp.int32)

    def one_device(item):
        count_row, start_row = item
        valid_slot = position[None, :] < count_row[:, None]
        row_index = jnp.where(valid_slot, start_row[:, None] + position[None, :], 0).astype(jnp.int32)
        rows = source_rows[sources[:, None], row_index]
        rows = jnp.where(valid_slot[:, :, None], rows.astype(jnp.float32), 0.0)
        row_mean = lax.optimization_barrier(jnp.mean(rows, axis=-1, keepdims=True))
        centred = rows - row_mean
        row_var = lax.optimization_barrier(jnp.mean(centred * centred, axis=-1, keepdims=True))
        normed = (centred * lax.rsqrt(row_var + 1e-06)).astype(jnp.bfloat16).reshape(IMG_DEV * MAXP, D)
        projected = [jnp.dot(normed, w_qkv[which].T, preferred_element_type=jnp.float32).astype(jnp.bfloat16).reshape(IMG_DEV, MAXP, HEADS, HD) for which in range(3)]
        query, key_rows, value = projected
        scores = jnp.einsum('sphd,sqhd->shpq', query.astype(jnp.float32), key_rows.astype(jnp.float32)) / math.sqrt(HD)
        scores = jnp.where(valid_slot[:, None, None, :], scores, -1e+30)
        row_max = lax.optimization_barrier(jnp.max(scores, axis=-1, keepdims=True))
        raised = jnp.exp(scores - row_max)
        weights = (raised / lax.optimization_barrier(jnp.sum(raised, axis=-1, keepdims=True))).astype(jnp.bfloat16)
        mixed = jnp.einsum('shpq,sqhd->sphd', weights.astype(jnp.float32), value.astype(jnp.float32)).astype(jnp.bfloat16).reshape(IMG_DEV, MAXP, D)
        counts_float = count_row.astype(jnp.float32)[:, None]
        pooled_heads = (lax.optimization_barrier(jnp.sum(jnp.where(valid_slot[:, :, None], mixed.astype(jnp.float32), 0.0), axis=1)) / counts_float).astype(jnp.bfloat16)
        pooled = lax.optimization_barrier(jnp.sum(rows, axis=1)) / counts_float + jnp.dot(pooled_heads, w_out, preferred_element_type=jnp.float32)
        scale_rows = lax.rsqrt(lax.optimization_barrier(jnp.sum(pooled * pooled, axis=-1, keepdims=True)) + 1e-06)
        return (pooled * scale_rows).astype(jnp.bfloat16)
    image_unit = lax.map(one_device, (got_count, got_start)).reshape(TOTAL, D)
    flat_ids = image_ids.reshape(TOTAL)
    text_float = text.astype(jnp.float32)
    text_unit = (text_float * lax.rsqrt(lax.optimization_barrier(jnp.sum(text_float * text_float, axis=-1, keepdims=True)) + 1e-06)).astype(jnp.bfloat16)
    logits = 4.0 * jnp.dot(image_unit, text_unit.T, preferred_element_type=jnp.float32) - 2.0
    labels = jnp.where(flat_ids[:, None] == jnp.arange(TOTAL, dtype=jnp.int32)[None, :], 1.0, -1.0)
    dscaled = (-4.0 * labels * jax.nn.sigmoid(-labels * logits)).astype(jnp.bfloat16)
    grad_image = jnp.dot(dscaled, text_unit, preferred_element_type=jnp.float32)
    grad_text = jnp.dot(dscaled.T, image_unit, preferred_element_type=jnp.float32)
    return (grad_image, grad_text)
```

```python
import functools
import math

import jax
import jax.numpy as jnp
from jax import lax
from jax.experimental import pallas as pl
from jax.experimental.pallas import tpu as pltpu
from jax.sharding import PartitionSpec as P

HD = 72
EPS = 1e-06
F32 = jnp.float32
BF16 = jnp.bfloat16
LAST_LAST = (((1,), (1,)), ((), ()))
FIRST_FIRST = (((0,), (0,)), ((), ()))


def dot(lhs, rhs, dims=(((1,), (0,)), ((), ()))):
    return lax.dot_general(lhs, rhs, dims, preferred_element_type=F32)


def iota(shape, dim):
    return lax.broadcasted_iota(jnp.int32, shape, dim)


def digits_of(peers):
    digits, stride = [], 1
    for factor in (2, 4, 3):
        while peers % factor == 0 and (factor != 2 or peers % 4):
            digits.append((stride, factor))
            stride, peers = stride * factor, peers // factor
    if peers > 1:
        digits.append((stride, peers))
    return digits[::-1]


def shifted(index, stride, radix, by):
    digit = index // stride % radix
    new = (digit + by) % radix if radix & (radix - 1) else digit ^ by
    return index + (new - digit) * stride


def moved(index, position, digits):
    place = 1
    for stride, radix in digits:
        index = shifted(index, stride, radix, position // place % radix)
        place *= radix
    return index


def fetch(block, axis, stride, radix, by):
    peers = lax.axis_size(axis)
    return lax.ppermute(block, axis, [(shifted(i, stride, radix, by), i) for i in range(peers)])


def load(images, *refs):
    sources, refs = refs[:6], refs[6:]
    *here, bias, member, spread, chosen, counts, dest, sems = refs
    copies = [
        pltpu.make_async_copy(source, target, sems.at[index])
        for index, (source, target) in enumerate(zip(sources, [counts, dest, *here]))
    ]
    for copy in copies:
        copy.start()
    for copy in copies[:2]:
        copy.wait()
    dp_index = lax.axis_index("dp")
    devices = chosen.shape[0]
    rows = member.shape[1]

    ends = []
    total = jnp.int32(0)
    for image in range(images):
        total = total + counts[dp_index * images + image]
        ends.append(total)

    def image_of(position):
        index = jnp.zeros(position.shape, jnp.int32)
        for end in ends:
            index = index + (position >= end).astype(jnp.int32)
        return index

    image_of_lane = image_of(iota((1, rows), 1))
    image_of_sublane = image_of(iota((rows, 1), 0))
    bias[...] = jnp.where(image_of_sublane == image_of_lane, 0.0, -1e30)
    belongs = (iota((images, rows), 0) == image_of_lane).astype(F32)
    member[...] = belongs
    heads = spread.shape[0] // images
    for head in range(heads):
        blocks = [belongs if other == head else jnp.zeros_like(belongs) for other in range(heads)]
        spread[head * images : (head + 1) * images, :] = jnp.concatenate(blocks, axis=1)

    target = moved(dp_index, iota((devices, images), 0), digits_of(devices))
    image = iota((devices, images), 1)
    goes = jnp.zeros((devices, images), F32)
    for index in range(images):
        here = (image == index) & (target == dest[dp_index * images + index])
        goes = jnp.where(here, 1.0, goes)
    chosen[...] = goes
    for copy in copies[2:]:
        copy.wait()


def attend(offsets, *refs):
    lanes = len(offsets)
    *pieces, bias, member, spread, w_qkv, w_out, share, patch_mean, x_rows = refs
    mp_index = lax.axis_index("mp")
    piece_width = pieces[0].shape[0]
    width, rows = x_rows.shape
    images = share.shape[0]
    local = w_qkv.shape[1]
    heads = local // HD

    for offset, piece in zip(offsets, pieces):
        start = moved(mp_index, offset, digits_of(lanes)) * piece_width
        x_rows[pl.ds(pl.multiple_of(start, 8), piece_width), :] = piece[...].astype(F32)
    x = x_rows[...]
    centred = x - jnp.sum(x, axis=0, keepdims=True) * (1.0 / width)
    variance = jnp.sum(centred * centred, axis=0, keepdims=True) * (1.0 / width)
    normed = (centred * lax.rsqrt(variance + EPS)).astype(BF16)
    query, key, value = (dot(w_qkv[which], normed) for which in range(3))

    belongs = member[...]
    count = jnp.sum(belongs, axis=1, keepdims=True)
    patch_mean[...] = dot(belongs.astype(BF16), x.astype(BF16), LAST_LAST) / count
    queries = []
    for head in range(heads):
        above, below = head * HD, (heads - 1 - head) * HD
        own = query[above : above + HD]
        blocks = [jnp.zeros((above, rows), F32)] * (above > 0) + [own]
        blocks += [jnp.zeros((below, rows), F32)] * (below > 0)
        queries.append(jnp.concatenate(blocks, axis=0))
    queries = jnp.concatenate(queries, axis=1).astype(BF16)
    scores = dot(key.T.astype(BF16), queries) * (1.0 / math.sqrt(HD))
    scores = scores + jnp.concatenate([bias[...]] * heads, axis=1)
    raised = jnp.exp(scores - jnp.max(scores, axis=0, keepdims=True))
    weights = (raised * (1.0 / jnp.sum(raised, axis=0, keepdims=True))).astype(BF16)
    pooling = dot(spread[...].astype(BF16), weights, LAST_LAST).astype(BF16)
    mixed = dot(pooling, value.astype(BF16), LAST_LAST)
    column_head = iota((images, local), 1) // HD
    pooled_heads = jnp.zeros((images, local), F32)
    for head in range(heads):
        block = mixed[head * images : (head + 1) * images]
        pooled_heads = jnp.where(column_head == head, block, pooled_heads)
    pooled_heads = (pooled_heads / count).astype(BF16)
    share[...] = dot(pooled_heads, w_out[...])


def join(*refs):
    first, *texts, share, message = refs
    texts = [first, *texts[::-1]]
    text = jnp.concatenate([text[...].astype(F32) for text in texts], axis=0)
    text = text * lax.rsqrt(jnp.sum(text * text, axis=1, keepdims=True) + EPS)
    message[...] = jnp.concatenate([text, share[...]], axis=0).astype(BF16)


def pair(lanes, *refs):
    chosen, patch_mean, share, own, *others, message = refs
    arrived = [own, *others[::-1]]
    devices = message.shape[0]
    dp_index = lax.axis_index("dp")
    mp_index = lax.axis_index("mp")
    images, width = patch_mean.shape
    group = arrived[0].shape[0] - images
    texts_here = group // devices
    slice_width = width // lanes
    part = message.shape[2] - width

    pooled = patch_mean[...] + share[...]
    for block in arrived[1:]:
        pooled = pooled + block[...].astype(F32)[group:]
    image_unit = (
        pooled * lax.rsqrt(jnp.sum(pooled * pooled, axis=1, keepdims=True) + EPS)
    ).astype(BF16)
    text_unit = jnp.concatenate([block[:group] for block in arrived], axis=0)

    def scaled(logits, image_dim, text_dim):
        image_id = dp_index * images + iota(logits.shape, image_dim)
        index = iota(logits.shape, text_dim)
        text_dp = moved(dp_index, index % group // texts_here, digits_of(devices))
        text_mp = moved(mp_index, index // group, digits_of(lanes))
        text_id = (text_dp * lanes + text_mp) * texts_here + index % texts_here
        label = jnp.where(image_id == text_id, 1.0, -1.0)
        logits = 4.0 * logits - 2.0
        return -4.0 * label * jax.nn.sigmoid(-label * logits)

    by_image = scaled(dot(image_unit, text_unit, LAST_LAST), 0, 1)
    by_text = scaled(dot(text_unit[:group], image_unit, LAST_LAST), 1, 0).astype(BF16)

    goes = chosen[...]
    rows = sum(goes[:, image : image + 1] * by_image[image : image + 1] for image in range(images))
    image_grad = dot(rows.astype(BF16), text_unit)
    own_columns = image_grad[:, :slice_width]
    for lane in range(1, lanes):
        block = image_grad[:, lane * slice_width : (lane + 1) * slice_width]
        own_columns = jnp.where(mp_index == lane, block, own_columns)
    text_grad = dot(by_text, image_unit)
    parts = [own_columns[:, which * part : (which + 1) * part] for which in range(texts_here)]
    for position in range(devices):
        first = position * texts_here
        row = [block[position : position + 1] for block in parts]
        both = [text_grad[first : first + texts_here], jnp.concatenate(row, axis=0)]
        target = moved(dp_index, position, digits_of(devices))
        message[target] = jnp.concatenate(both, axis=1).astype(BF16)


def collect(message, image_grad, text_grad):
    texts_here, width = text_grad.shape
    part = message.shape[2] - width
    arrived = message[...].astype(F32)
    text_grad[...] = jnp.sum(arrived[:, :, :width], axis=0)
    for which in range(texts_here):
        columns = slice(which * part, (which + 1) * part)
        for source in range(arrived.shape[0]):
            image_grad[source : source + 1, columns] = arrived[source, which : which + 1, width:]


def call(kernel, out_shape, args, spaces=None, scratch=(), cost=None):
    spaces = spaces or [pltpu.VMEM] * len(args)
    return pl.pallas_call(
        kernel,
        out_shape=out_shape,
        in_specs=[pl.BlockSpec(memory_space=space) for space in spaces],
        out_specs=jax.tree.map(lambda _: pl.BlockSpec(memory_space=pltpu.VMEM), out_shape),
        scratch_shapes=scratch,
        cost_estimate=cost,
        compiler_params=pltpu.CompilerParams(vmem_limit_bytes=32 * 2**20),
    )(*args)


def on_device(patches, counts, dest, w_qkv, w_out, text):
    devices = lax.axis_size("dp")
    lanes = lax.axis_size("mp")
    images = counts.shape[0] // devices
    width = w_qkv.shape[2]
    rows = patches.shape[1]
    texts_here = text.shape[0]
    slice_width = width // lanes
    heads = w_qkv.shape[1] // HD
    dp_digits, mp_digits = digits_of(devices), digits_of(lanes)
    shape = jax.ShapeDtypeStruct

    sources = [counts, dest, patches, w_qkv, w_out, text]
    patches_here, w_qkv_here, w_out_here, text_here, bias, member, spread, chosen = call(
        functools.partial(load, images),
        (
            *(shape(source.shape, source.dtype) for source in sources[2:]),
            shape((rows, rows), F32),
            shape((images, rows), F32),
            shape((heads * images, heads * rows), F32),
            shape((devices, images), F32),
        ),
        [pltpu.with_memory_space_constraint(source, pltpu.HBM) for source in sources],
        [pltpu.HBM] * 6,
        scratch=[
            pltpu.SMEM(counts.shape, jnp.int32),
            pltpu.SMEM(dest.shape, jnp.int32),
            pltpu.SemaphoreType.DMA((6,)),
        ],
        cost=pl.CostEstimate(flops=0, bytes_accessed=6 * w_qkv.size, transcendentals=0),
    )

    offsets = range(lanes)
    pieces = [
        lax.ppermute(patches, "mp", [(moved(i, offset, mp_digits), i) for i in range(lanes)])
        for offset in offsets[1:]
    ]
    texts = [text_here]
    for stride, radix in dp_digits:
        block = jnp.concatenate(texts, axis=0)
        sent = block if len(texts) > 1 else text
        texts = [block] + [fetch(sent, "dp", stride, radix, by) for by in range(1, radix)]

    share, patch_mean = call(
        functools.partial(attend, offsets),
        (shape((images, width), F32), shape((images, width), F32)),
        [patches_here, *pieces, bias, member, spread, w_qkv_here, w_out_here],
        scratch=[pltpu.VMEM((width, rows), F32)],
    )
    texts = [texts[0], *texts[:0:-1]]
    message = call(join, shape((devices * texts_here + images, width), BF16), [*texts, share])
    arrived = [message] + [
        lax.ppermute(message, "mp", [(moved(i, offset, mp_digits), i) for i in range(lanes)])
        for offset in offsets[1:]
    ]
    message = call(
        functools.partial(pair, lanes),
        shape((devices, texts_here, width + slice_width // texts_here), BF16),
        [chosen, patch_mean, share, arrived[0], *arrived[:0:-1]],
    )
    message = lax.all_to_all(message, "dp", split_axis=0, concat_axis=0, tiled=True)
    return call(
        collect,
        (shape((devices, slice_width), F32), shape((texts_here, width), F32)),
        [message],
    )


def solution(mesh):
    placed = (P("mp", "dp"), P(), P(), P(None, "mp", None), P("mp", None), P(("dp", "mp"), None))
    return jax.shard_map(
        on_device,
        mesh=mesh,
        in_specs=placed,
        out_specs=(P("dp", "mp"), P(("dp", "mp"), None)),
        check_vma=False,
    )
```

```python
import functools
import math

import jax
import jax.numpy as jnp
from jax import lax
from jax.experimental import pallas as pl
from jax.experimental.pallas import tpu as pltpu
from jax.sharding import PartitionSpec as P

HD = 72
EPS = 1e-06
F32 = jnp.float32
BF16 = jnp.bfloat16
LAST_LAST = (((1,), (1,)), ((), ()))
FIRST_FIRST = (((0,), (0,)), ((), ()))


def dot(lhs, rhs, dims=(((1,), (0,)), ((), ()))):
    return lax.dot_general(lhs, rhs, dims, preferred_element_type=F32)


def iota(shape, dim):
    return lax.broadcasted_iota(jnp.int32, shape, dim)


def digits_of(peers):
    digits, stride = [], 1
    for factor in (2, 4, 3):
        while peers % factor == 0 and (factor != 2 or peers % 4):
            digits.append((stride, factor))
            stride, peers = stride * factor, peers // factor
    if peers > 1:
        digits.append((stride, peers))
    return digits[::-1]


def shifted(index, stride, radix, by):
    digit = index // stride % radix
    new = (digit + by) % radix if radix & (radix - 1) else digit ^ by
    return index + (new - digit) * stride


def moved(index, position, digits):
    place = 1
    for stride, radix in digits:
        index = shifted(index, stride, radix, position // place % radix)
        place *= radix
    return index


def fetch(block, axis, stride, radix, by):
    peers = lax.axis_size(axis)
    return lax.ppermute(block, axis, [(shifted(i, stride, radix, by), i) for i in range(peers)])


def load(images, *refs):
    sources, refs = refs[:6], refs[6:]
    *here, bias, member, spread, chosen, counts, dest, sems = refs
    copies = [
        pltpu.make_async_copy(source, target, sems.at[index])
        for index, (source, target) in enumerate(zip(sources, [counts, dest, *here]))
    ]
    for copy in copies:
        copy.start()
    for copy in copies[:2]:
        copy.wait()
    dp_index = lax.axis_index("dp")
    devices = chosen.shape[0]
    rows = member.shape[1]

    ends = []
    total = jnp.int32(0)
    for image in range(images):
        total = total + counts[dp_index * images + image]
        ends.append(total)

    def image_of(position):
        index = jnp.zeros(position.shape, jnp.int32)
        for end in ends:
            index = index + (position >= end).astype(jnp.int32)
        return index

    image_of_lane = image_of(iota((1, rows), 1))
    image_of_sublane = image_of(iota((rows, 1), 0))
    bias[...] = jnp.where(image_of_sublane == image_of_lane, 0.0, -1e30)
    belongs = (iota((images, rows), 0) == image_of_lane).astype(F32)
    member[...] = belongs
    heads = spread.shape[0] // images
    for head in range(heads):
        blocks = [belongs if other == head else jnp.zeros_like(belongs) for other in range(heads)]
        spread[head * images : (head + 1) * images, :] = jnp.concatenate(blocks, axis=1)

    target = moved(dp_index, iota((devices, images), 0), digits_of(devices))
    image = iota((devices, images), 1)
    goes = jnp.zeros((devices, images), F32)
    for index in range(images):
        here = (image == index) & (target == dest[dp_index * images + index])
        goes = jnp.where(here, 1.0, goes)
    chosen[...] = goes
    for copy in copies[2:]:
        copy.wait()


def attend(offsets, *refs):
    lanes = len(offsets)
    *pieces, bias, member, spread, w_qkv, w_out, share, patch_mean, x_rows = refs
    mp_index = lax.axis_index("mp")
    piece_width = pieces[0].shape[0]
    width, rows = x_rows.shape
    images = share.shape[0]
    local = w_qkv.shape[1]
    heads = local // HD

    for offset, piece in zip(offsets, pieces):
        start = moved(mp_index, offset, digits_of(lanes)) * piece_width
        x_rows[pl.ds(pl.multiple_of(start, 8), piece_width), :] = piece[...].astype(F32)
    x = x_rows[...]
    centred = x - jnp.sum(x, axis=0, keepdims=True) * (1.0 / width)
    variance = jnp.sum(centred * centred, axis=0, keepdims=True) * (1.0 / width)
    normed = (centred * lax.rsqrt(variance + EPS)).astype(BF16)
    query, key, value = (dot(w_qkv[which], normed) for which in range(3))

    belongs = member[...]
    count = jnp.sum(belongs, axis=1, keepdims=True)
    patch_mean[...] = dot(belongs.astype(BF16), x.astype(BF16), LAST_LAST) / count
    row_head = iota(query.shape, 0) // HD
    queries = [jnp.where(row_head == head, query, 0.0) for head in range(heads)]
    queries = jnp.concatenate(queries, axis=1).astype(BF16)
    scores = dot(key.T.astype(BF16), queries) * (1.0 / math.sqrt(HD))
    same = jnp.concatenate([bias[...]] * heads, axis=1) > -1.0
    scores = jnp.where(same, scores, -1e30)
    raised = jnp.exp(scores - jnp.max(scores, axis=0, keepdims=True))
    weights = (raised * (1.0 / jnp.sum(raised, axis=0, keepdims=True))).astype(BF16)
    pooling = dot(spread[...].astype(BF16), weights, LAST_LAST).astype(BF16)
    mixed = dot(pooling, value.astype(BF16), LAST_LAST)
    column_head = iota((images, local), 1) // HD
    pooled_heads = jnp.zeros((images, local), F32)
    for head in range(heads):
        block = mixed[head * images : (head + 1) * images]
        pooled_heads = jnp.where(column_head == head, block, pooled_heads)
    pooled_heads = (pooled_heads / count).astype(BF16)
    share[...] = dot(pooled_heads, w_out[...])


def join(*refs):
    first, *texts, share, message = refs
    texts = [first, *texts[::-1]]
    text = jnp.concatenate([text[...].astype(F32) for text in texts], axis=0)
    text = text * lax.rsqrt(jnp.sum(text * text, axis=1, keepdims=True) + EPS)
    message[...] = jnp.concatenate([text, share[...]], axis=0).astype(BF16)


def pair(lanes, *refs):
    chosen, patch_mean, share, own, *others, message = refs
    arrived = [own, *others[::-1]]
    devices = message.shape[0]
    dp_index = lax.axis_index("dp")
    mp_index = lax.axis_index("mp")
    images, width = patch_mean.shape
    group = arrived[0].shape[0] - images
    texts_here = group // devices
    slice_width = width // lanes
    part = message.shape[2] - width

    pooled = patch_mean[...] + share[...]
    for block in arrived[1:]:
        pooled = pooled + block[...].astype(F32)[group:]
    image_unit = (
        pooled * lax.rsqrt(jnp.sum(pooled * pooled, axis=1, keepdims=True) + EPS)
    ).astype(BF16)
    text_unit = jnp.concatenate([block[:group] for block in arrived], axis=0)

    def scaled(logits, image_dim, text_dim):
        image_id = dp_index * images + iota(logits.shape, image_dim)
        index = iota(logits.shape, text_dim)
        text_dp = moved(dp_index, index % group // texts_here, digits_of(devices))
        text_mp = moved(mp_index, index // group, digits_of(lanes))
        text_id = (text_dp * lanes + text_mp) * texts_here + index % texts_here
        label = jnp.where(image_id == text_id, 1.0, -1.0)
        logits = 4.0 * logits - 2.0
        return -4.0 * label * jax.nn.sigmoid(-label * logits)

    own_columns = text_unit[:, :slice_width]
    for lane in range(1, lanes):
        block = text_unit[:, lane * slice_width : (lane + 1) * slice_width]
        own_columns = jnp.where(mp_index == lane, block, own_columns)
    by_image = scaled(dot(image_unit, text_unit, LAST_LAST), 0, 1)
    text_grad = dot(by_image[:, :group].astype(BF16), image_unit, FIRST_FIRST)
    goes = chosen[...]
    rows = sum(goes[:, image : image + 1] * by_image[image : image + 1] for image in range(images))
    image_grad = dot(rows.astype(BF16), own_columns)
    parts = [image_grad[:, which * part : (which + 1) * part] for which in range(texts_here)]
    for position in range(devices):
        first = position * texts_here
        row = [block[position : position + 1] for block in parts]
        both = [text_grad[first : first + texts_here], jnp.concatenate(row, axis=0)]
        target = moved(dp_index, position, digits_of(devices))
        message[target] = jnp.concatenate(both, axis=1).astype(BF16)


def collect(message, image_grad, text_grad):
    texts_here, width = text_grad.shape
    part = message.shape[2] - width
    arrived = message[...].astype(F32)
    text_grad[...] = jnp.sum(arrived[:, :, :width], axis=0)
    for which in range(texts_here):
        columns = slice(which * part, (which + 1) * part)
        for source in range(arrived.shape[0]):
            image_grad[source : source + 1, columns] = arrived[source, which : which + 1, width:]


def call(kernel, out_shape, args, spaces=None, scratch=(), cost=None):
    spaces = spaces or [pltpu.VMEM] * len(args)
    return pl.pallas_call(
        kernel,
        out_shape=out_shape,
        in_specs=[pl.BlockSpec(memory_space=space) for space in spaces],
        out_specs=jax.tree.map(lambda _: pl.BlockSpec(memory_space=pltpu.VMEM), out_shape),
        scratch_shapes=scratch,
        cost_estimate=cost,
        compiler_params=pltpu.CompilerParams(vmem_limit_bytes=32 * 2**20),
    )(*args)


def on_device(patches, counts, dest, w_qkv, w_out, text):
    devices = lax.axis_size("dp")
    lanes = lax.axis_size("mp")
    images = counts.shape[0] // devices
    width = w_qkv.shape[2]
    rows = patches.shape[1]
    texts_here = text.shape[0]
    slice_width = width // lanes
    heads = w_qkv.shape[1] // HD
    dp_digits, mp_digits = digits_of(devices), digits_of(lanes)
    shape = jax.ShapeDtypeStruct

    sources = [counts, dest, patches, w_qkv, w_out, text]
    patches_here, w_qkv_here, w_out_here, text_here, bias, member, spread, chosen = call(
        functools.partial(load, images),
        (
            *(shape(source.shape, source.dtype) for source in sources[2:]),
            shape((rows, rows), F32),
            shape((images, rows), F32),
            shape((heads * images, heads * rows), F32),
            shape((devices, images), F32),
        ),
        [pltpu.with_memory_space_constraint(source, pltpu.HBM) for source in sources],
        [pltpu.HBM] * 6,
        scratch=[
            pltpu.SMEM(counts.shape, jnp.int32),
            pltpu.SMEM(dest.shape, jnp.int32),
            pltpu.SemaphoreType.DMA((6,)),
        ],
        cost=pl.CostEstimate(flops=0, bytes_accessed=6 * w_qkv.size, transcendentals=0),
    )

    offsets = range(lanes)
    pieces = [
        lax.ppermute(patches, "mp", [(moved(i, offset, mp_digits), i) for i in range(lanes)])
        for offset in offsets[1:]
    ]
    texts = [text_here]
    for stride, radix in dp_digits:
        block = jnp.concatenate(texts, axis=0)
        sent = block if len(texts) > 1 else text
        texts = [block] + [fetch(sent, "dp", stride, radix, by) for by in range(1, radix)]

    share, patch_mean = call(
        functools.partial(attend, offsets),
        (shape((images, width), F32), shape((images, width), F32)),
        [patches_here, *pieces, bias, member, spread, w_qkv_here, w_out_here],
        scratch=[pltpu.VMEM((width, rows), F32)],
    )
    texts = [texts[0], *texts[:0:-1]]
    message = call(join, shape((devices * texts_here + images, width), BF16), [*texts, share])
    arrived = [message] + [
        lax.ppermute(message, "mp", [(moved(i, offset, mp_digits), i) for i in range(lanes)])
        for offset in offsets[1:]
    ]
    message = call(
        functools.partial(pair, lanes),
        shape((devices, texts_here, width + slice_width // texts_here), BF16),
        [chosen, patch_mean, share, arrived[0], *arrived[:0:-1]],
    )
    message = lax.all_to_all(message, "dp", split_axis=0, concat_axis=0, tiled=True)
    return call(
        collect,
        (shape((devices, slice_width), F32), shape((texts_here, width), F32)),
        [message],
    )


def solution(mesh):
    placed = (P("mp", "dp"), P(), P(), P(None, "mp", None), P("mp", None), P(("dp", "mp"), None))
    return jax.shard_map(
        on_device,
        mesh=mesh,
        in_specs=placed,
        out_specs=(P("dp", "mp"), P(("dp", "mp"), None)),
        check_vma=False,
    )
```

```python
import functools
import math

import jax
import jax.numpy as jnp
from jax import lax
from jax.experimental import pallas as pl
from jax.experimental.pallas import tpu as pltpu
from jax.sharding import PartitionSpec as P

HD = 72
EPS = 1e-06
F32 = jnp.float32
BF16 = jnp.bfloat16
LAST_LAST = (((1,), (1,)), ((), ()))
FIRST_FIRST = (((0,), (0,)), ((), ()))


def dot(lhs, rhs, dims=(((1,), (0,)), ((), ()))):
    return lax.dot_general(lhs, rhs, dims, preferred_element_type=F32)


def iota(shape, dim):
    return lax.broadcasted_iota(jnp.int32, shape, dim)


def digits_of(peers):
    digits, stride = [], 1
    for factor in (2, 4, 3):
        while peers % factor == 0 and (factor != 2 or peers % 4):
            digits.append((stride, factor))
            stride, peers = stride * factor, peers // factor
    if peers > 1:
        digits.append((stride, peers))
    return digits[::-1]


def shifted(index, stride, radix, by):
    digit = index // stride % radix
    new = (digit + by) % radix if radix & (radix - 1) else digit ^ by
    return index + (new - digit) * stride


def moved(index, position, digits):
    place = 1
    for stride, radix in digits:
        index = shifted(index, stride, radix, position // place % radix)
        place *= radix
    return index


def fetch(block, axis, stride, radix, by):
    peers = lax.axis_size(axis)
    return lax.ppermute(block, axis, [(shifted(i, stride, radix, by), i) for i in range(peers)])


def load(images, *refs):
    sources, refs = refs[:6], refs[6:]
    *here, bias, member, spread, chosen, counts, dest, sems = refs
    copies = [
        pltpu.make_async_copy(source, target, sems.at[index])
        for index, (source, target) in enumerate(zip(sources, [counts, dest, *here]))
    ]
    for copy in copies:
        copy.start()
    for copy in copies[:2]:
        copy.wait()
    dp_index = lax.axis_index("dp")
    devices = chosen.shape[0]
    rows = member.shape[1]

    ends = []
    total = jnp.int32(0)
    for image in range(images):
        total = total + counts[dp_index * images + image]
        ends.append(total)

    def image_of(position):
        index = jnp.zeros(position.shape, jnp.int32)
        for end in ends:
            index = index + (position >= end).astype(jnp.int32)
        return index

    image_of_lane = image_of(iota((1, rows), 1))
    image_of_sublane = image_of(iota((rows, 1), 0))
    bias[...] = jnp.where(image_of_sublane == image_of_lane, 0.0, -1e30)
    belongs = (iota((images, rows), 0) == image_of_lane).astype(F32)
    member[...] = belongs
    heads = spread.shape[0] // images
    for head in range(heads):
        blocks = [belongs if other == head else jnp.zeros_like(belongs) for other in range(heads)]
        spread[head * images : (head + 1) * images, :] = jnp.concatenate(blocks, axis=1)

    target = moved(dp_index, iota((devices, images), 0), digits_of(devices))
    image = iota((devices, images), 1)
    goes = jnp.zeros((devices, images), F32)
    for index in range(images):
        here = (image == index) & (target == dest[dp_index * images + index])
        goes = jnp.where(here, 1.0, goes)
    chosen[...] = goes
    for copy in copies[2:]:
        copy.wait()


def attend(offsets, *refs):
    lanes = len(offsets)
    *pieces, bias, member, spread, w_qkv, w_out, share, patch_rows, x_rows = refs
    mp_index = lax.axis_index("mp")
    piece_width = pieces[0].shape[0]
    width, rows = x_rows.shape
    images = share.shape[0]
    local = w_qkv.shape[1]
    heads = local // HD

    for offset, piece in zip(offsets, pieces):
        start = moved(mp_index, offset, digits_of(lanes)) * piece_width
        x_rows[pl.ds(pl.multiple_of(start, 8), piece_width), :] = piece[...].astype(F32)
    x = x_rows[...]
    centred = x - jnp.sum(x, axis=0, keepdims=True) * (1.0 / width)
    variance = jnp.sum(centred * centred, axis=0, keepdims=True) * (1.0 / width)
    normed = (centred * lax.rsqrt(variance + EPS)).astype(BF16)
    query, key, value = (dot(w_qkv[which], normed) for which in range(3))

    belongs = member[...]
    count = jnp.sum(belongs, axis=1, keepdims=True)
    patch_rows[...] = x.astype(BF16)
    row_head = iota(query.shape, 0) // HD
    queries = [jnp.where(row_head == head, query, 0.0) for head in range(heads)]
    queries = jnp.concatenate(queries, axis=1).astype(BF16)
    scores = dot(key.T.astype(BF16), queries) * (1.0 / math.sqrt(HD))
    same = jnp.concatenate([bias[...]] * heads, axis=1) > -1.0
    scores = jnp.where(same, scores, -1e30)
    raised = jnp.exp(scores - jnp.max(scores, axis=0, keepdims=True))
    weights = (raised * (1.0 / jnp.sum(raised, axis=0, keepdims=True))).astype(BF16)
    pooling = dot(spread[...].astype(BF16), weights, LAST_LAST).astype(BF16)
    mixed = dot(pooling, value.astype(BF16), LAST_LAST)
    column_head = iota((images, local), 1) // HD
    pooled_heads = jnp.zeros((images, local), F32)
    for head in range(heads):
        block = mixed[head * images : (head + 1) * images]
        pooled_heads = jnp.where(column_head == head, block, pooled_heads)
    pooled_heads = (pooled_heads / count).astype(BF16)
    share[...] = dot(pooled_heads, w_out[...])


def average(member, patch_rows, patch_mean):
    belongs = member[...]
    count = jnp.sum(belongs, axis=1, keepdims=True)
    patch_mean[...] = dot(belongs.astype(BF16), patch_rows[...], LAST_LAST) / count


def join(*refs):
    first, *texts, share, message = refs
    texts = [first, *texts[::-1]]
    text = jnp.concatenate([text[...].astype(F32) for text in texts], axis=0)
    text = text * lax.rsqrt(jnp.sum(text * text, axis=1, keepdims=True) + EPS)
    message[...] = jnp.concatenate([text, share[...]], axis=0).astype(BF16)


def pair(lanes, *refs):
    chosen, patch_mean, share, own, *others, message = refs
    arrived = [own, *others[::-1]]
    devices = message.shape[0]
    dp_index = lax.axis_index("dp")
    mp_index = lax.axis_index("mp")
    images, width = patch_mean.shape
    group = arrived[0].shape[0] - images
    texts_here = group // devices
    slice_width = width // lanes
    part = message.shape[2] - width

    pooled = patch_mean[...] + share[...]
    for block in arrived[1:]:
        pooled = pooled + block[...].astype(F32)[group:]
    image_unit = (
        pooled * lax.rsqrt(jnp.sum(pooled * pooled, axis=1, keepdims=True) + EPS)
    ).astype(BF16)
    text_unit = jnp.concatenate([block[:group] for block in arrived], axis=0)

    def scaled(logits, image_dim, text_dim):
        image_id = dp_index * images + iota(logits.shape, image_dim)
        index = iota(logits.shape, text_dim)
        text_dp = moved(dp_index, index % group // texts_here, digits_of(devices))
        text_mp = moved(mp_index, index // group, digits_of(lanes))
        text_id = (text_dp * lanes + text_mp) * texts_here + index % texts_here
        label = jnp.where(image_id == text_id, 1.0, -1.0)
        logits = 4.0 * logits - 2.0
        return -4.0 * label * jax.nn.sigmoid(-label * logits)

    own_columns = text_unit[:, :slice_width]
    for lane in range(1, lanes):
        block = text_unit[:, lane * slice_width : (lane + 1) * slice_width]
        own_columns = jnp.where(mp_index == lane, block, own_columns)
    by_image = scaled(dot(image_unit, text_unit, LAST_LAST), 0, 1)
    text_grad = dot(by_image[:, :group].astype(BF16), image_unit, FIRST_FIRST)
    goes = chosen[...]
    rows = sum(goes[:, image : image + 1] * by_image[image : image + 1] for image in range(images))
    image_grad = dot(rows.astype(BF16), own_columns)
    parts = [image_grad[:, which * part : (which + 1) * part] for which in range(texts_here)]
    for position in range(devices):
        first = position * texts_here
        row = [block[position : position + 1] for block in parts]
        both = [text_grad[first : first + texts_here], jnp.concatenate(row, axis=0)]
        target = moved(dp_index, position, digits_of(devices))
        message[target] = jnp.concatenate(both, axis=1).astype(BF16)


def collect(message, image_grad, text_grad):
    texts_here, width = text_grad.shape
    part = message.shape[2] - width
    arrived = message[...].astype(F32)
    text_grad[...] = jnp.sum(arrived[:, :, :width], axis=0)
    for which in range(texts_here):
        columns = slice(which * part, (which + 1) * part)
        for source in range(arrived.shape[0]):
            image_grad[source : source + 1, columns] = arrived[source, which : which + 1, width:]


def call(kernel, out_shape, args, spaces=None, scratch=(), cost=None):
    spaces = spaces or [pltpu.VMEM] * len(args)
    return pl.pallas_call(
        kernel,
        out_shape=out_shape,
        in_specs=[pl.BlockSpec(memory_space=space) for space in spaces],
        out_specs=jax.tree.map(lambda _: pl.BlockSpec(memory_space=pltpu.VMEM), out_shape),
        scratch_shapes=scratch,
        cost_estimate=cost,
        compiler_params=pltpu.CompilerParams(vmem_limit_bytes=32 * 2**20),
    )(*args)


def on_device(patches, counts, dest, w_qkv, w_out, text):
    devices = lax.axis_size("dp")
    lanes = lax.axis_size("mp")
    images = counts.shape[0] // devices
    width = w_qkv.shape[2]
    rows = patches.shape[1]
    texts_here = text.shape[0]
    slice_width = width // lanes
    heads = w_qkv.shape[1] // HD
    dp_digits, mp_digits = digits_of(devices), digits_of(lanes)
    shape = jax.ShapeDtypeStruct

    sources = [counts, dest, patches, w_qkv, w_out, text]
    patches_here, w_qkv_here, w_out_here, text_here, bias, member, spread, chosen = call(
        functools.partial(load, images),
        (
            *(shape(source.shape, source.dtype) for source in sources[2:]),
            shape((rows, rows), F32),
            shape((images, rows), F32),
            shape((heads * images, heads * rows), F32),
            shape((devices, images), F32),
        ),
        [pltpu.with_memory_space_constraint(source, pltpu.HBM) for source in sources],
        [pltpu.HBM] * 6,
        scratch=[
            pltpu.SMEM(counts.shape, jnp.int32),
            pltpu.SMEM(dest.shape, jnp.int32),
            pltpu.SemaphoreType.DMA((6,)),
        ],
        cost=pl.CostEstimate(flops=0, bytes_accessed=6 * w_qkv.size, transcendentals=0),
    )

    offsets = range(lanes)
    pieces = [
        lax.ppermute(patches, "mp", [(moved(i, offset, mp_digits), i) for i in range(lanes)])
        for offset in offsets[1:]
    ]
    texts = [text_here]
    for stride, radix in dp_digits:
        block = jnp.concatenate(texts, axis=0)
        sent = block if len(texts) > 1 else text
        texts = [block] + [fetch(sent, "dp", stride, radix, by) for by in range(1, radix)]

    share, patch_rows = call(
        functools.partial(attend, offsets),
        (shape((images, width), F32), shape((width, rows), BF16)),
        [patches_here, *pieces, bias, member, spread, w_qkv_here, w_out_here],
        scratch=[pltpu.VMEM((width, rows), F32)],
    )
    patch_mean = call(
        average,
        shape((images, width), F32),
        [member, patch_rows],
        cost=pl.CostEstimate(flops=10**9, bytes_accessed=0, transcendentals=0),
    )
    texts = [texts[0], *texts[:0:-1]]
    message = call(join, shape((devices * texts_here + images, width), BF16), [*texts, share])
    arrived = [message] + [
        lax.ppermute(message, "mp", [(moved(i, offset, mp_digits), i) for i in range(lanes)])
        for offset in offsets[1:]
    ]
    message = call(
        functools.partial(pair, lanes),
        shape((devices, texts_here, width + slice_width // texts_here), BF16),
        [chosen, patch_mean, share, arrived[0], *arrived[:0:-1]],
    )
    message = lax.all_to_all(message, "dp", split_axis=0, concat_axis=0, tiled=True)
    return call(
        collect,
        (shape((devices, slice_width), F32), shape((texts_here, width), F32)),
        [message],
    )


def solution(mesh):
    placed = (P("mp", "dp"), P(), P(), P(None, "mp", None), P("mp", None), P(("dp", "mp"), None))
    return jax.shard_map(
        on_device,
        mesh=mesh,
        in_specs=placed,
        out_specs=(P("dp", "mp"), P(("dp", "mp"), None)),
        check_vma=False,
    )
```

```python
import functools
import math

import jax
import jax.numpy as jnp
from jax import lax
from jax.experimental import pallas as pl
from jax.experimental.pallas import tpu as pltpu
from jax.sharding import PartitionSpec as P

HD = 72
EPS = 1e-06
F32 = jnp.float32
BF16 = jnp.bfloat16
LAST_LAST = (((1,), (1,)), ((), ()))
FIRST_FIRST = (((0,), (0,)), ((), ()))


def dot(lhs, rhs, dims=(((1,), (0,)), ((), ()))):
    return lax.dot_general(lhs, rhs, dims, preferred_element_type=F32)


def iota(shape, dim):
    return lax.broadcasted_iota(jnp.int32, shape, dim)


def digits_of(peers):
    digits, stride = [], 1
    for factor in (2, 4, 3):
        while peers % factor == 0 and (factor != 2 or peers % 4):
            digits.append((stride, factor))
            stride, peers = stride * factor, peers // factor
    if peers > 1:
        digits.append((stride, peers))
    return digits[::-1]


def shifted(index, stride, radix, by):
    digit = index // stride % radix
    new = (digit + by) % radix if radix & (radix - 1) else digit ^ by
    return index + (new - digit) * stride


def moved(index, position, digits):
    place = 1
    for stride, radix in digits:
        index = shifted(index, stride, radix, position // place % radix)
        place *= radix
    return index


def fetch(block, axis, stride, radix, by):
    peers = lax.axis_size(axis)
    return lax.ppermute(block, axis, [(shifted(i, stride, radix, by), i) for i in range(peers)])


def load(images, *refs):
    sources, refs = refs[:6], refs[6:]
    *here, bias, member, spread, chosen, counts, dest, sems = refs
    copies = [
        pltpu.make_async_copy(source, target, sems.at[index])
        for index, (source, target) in enumerate(zip(sources, [counts, dest, *here]))
    ]
    for copy in copies:
        copy.start()
    for copy in copies[:2]:
        copy.wait()
    dp_index = lax.axis_index("dp")
    devices = chosen.shape[0]
    rows = member.shape[1]

    ends = []
    total = jnp.int32(0)
    for image in range(images):
        total = total + counts[dp_index * images + image]
        ends.append(total)

    def image_of(position):
        index = jnp.zeros(position.shape, jnp.int32)
        for end in ends:
            index = index + (position >= end).astype(jnp.int32)
        return index

    image_of_lane = image_of(iota((1, rows), 1))
    image_of_sublane = image_of(iota((rows, 1), 0))
    bias[...] = jnp.where(image_of_sublane == image_of_lane, 0.0, -1e30)
    belongs = (iota((images, rows), 0) == image_of_lane).astype(F32)
    member[...] = belongs
    heads = spread.shape[0] // images
    for head in range(heads):
        blocks = [belongs if other == head else jnp.zeros_like(belongs) for other in range(heads)]
        spread[head * images : (head + 1) * images, :] = jnp.concatenate(blocks, axis=1)

    target = moved(dp_index, iota((devices, images), 0), digits_of(devices))
    image = iota((devices, images), 1)
    goes = jnp.zeros((devices, images), F32)
    for index in range(images):
        here = (image == index) & (target == dest[dp_index * images + index])
        goes = jnp.where(here, 1.0, goes)
    chosen[...] = goes
    for copy in copies[2:]:
        copy.wait()


def attend(offsets, *refs):
    lanes = len(offsets)
    *pieces, bias, member, spread, w_qkv, w_out, share, patch_rows, x_rows = refs
    mp_index = lax.axis_index("mp")
    piece_width = pieces[0].shape[0]
    width, rows = x_rows.shape
    images = share.shape[0]
    local = w_qkv.shape[1]
    heads = local // HD

    for offset, piece in zip(offsets, pieces):
        start = moved(mp_index, offset, digits_of(lanes)) * piece_width
        x_rows[pl.ds(pl.multiple_of(start, 8), piece_width), :] = piece[...].astype(F32)
    x = x_rows[...]
    centred = x - jnp.sum(x, axis=0, keepdims=True) * (1.0 / width)
    variance = jnp.sum(centred * centred, axis=0, keepdims=True) * (1.0 / width)
    normed = (centred * lax.rsqrt(variance + EPS)).astype(BF16)
    query, key, value = (dot(w_qkv[which], normed) for which in range(3))

    belongs = member[...]
    count = jnp.sum(belongs, axis=1, keepdims=True)
    patch_rows[...] = x.astype(BF16)
    row_head = iota(query.shape, 0) // HD
    queries = [jnp.where(row_head == head, query, 0.0) for head in range(heads)]
    queries = jnp.concatenate(queries, axis=1).astype(BF16)
    scores = dot(key.T.astype(BF16), queries) * (1.0 / math.sqrt(HD))
    same = jnp.concatenate([bias[...]] * heads, axis=1) > -1.0
    scores = jnp.where(same, scores, -1e30)
    raised = jnp.exp(scores - jnp.max(scores, axis=0, keepdims=True))
    weights = (raised * (1.0 / jnp.sum(raised, axis=0, keepdims=True))).astype(BF16)
    pooling = dot(spread[...].astype(BF16), weights, LAST_LAST).astype(BF16)
    mixed = dot(pooling, value.astype(BF16), LAST_LAST)
    column_head = iota((images, local), 1) // HD
    pooled_heads = jnp.zeros((images, local), F32)
    for head in range(heads):
        block = mixed[head * images : (head + 1) * images]
        pooled_heads = jnp.where(column_head == head, block, pooled_heads)
    pooled_heads = (pooled_heads / count).astype(BF16)
    share[...] = dot(pooled_heads, w_out[...])


def average(lanes, devices, texts_here, member, chosen, share, patch_rows, pooled, label, order):
    belongs = member[...]
    count = jnp.sum(belongs, axis=1, keepdims=True)
    patch_mean = dot(belongs.astype(BF16), patch_rows[...], LAST_LAST) / count
    pooled[...] = patch_mean + share[...]

    dp_index = lax.axis_index("dp")
    mp_index = lax.axis_index("mp")
    images, texts = label.shape
    group = devices * texts_here
    image_id = dp_index * images + iota((images, texts), 0)
    index = iota((images, texts), 1)
    text_dp = moved(dp_index, index % group // texts_here, digits_of(devices))
    text_mp = moved(mp_index, index // group, digits_of(lanes))
    text_id = (text_dp * lanes + text_mp) * texts_here + index % texts_here
    label[...] = jnp.where(image_id == text_id, 1.0, -1.0)
    goes = chosen[...]
    for image in range(images):
        order[image] = jnp.broadcast_to(goes[:, image : image + 1], order.shape[1:])


def join(*refs):
    first, *texts, share, message = refs
    texts[:2] = texts[1::-1]
    texts = [first, *texts[::-1]]
    text = jnp.concatenate([text[...].astype(F32) for text in texts], axis=0)
    text = text * lax.rsqrt(jnp.sum(text * text, axis=1, keepdims=True) + EPS)
    message[...] = jnp.concatenate([text, share[...]], axis=0).astype(BF16)


def pair(lanes, *refs):
    pooled, label, order, own, *others, message = refs
    arrived = [own, *others[::-1]]
    devices = message.shape[0]
    dp_index = lax.axis_index("dp")
    mp_index = lax.axis_index("mp")
    images, width = pooled.shape
    group = arrived[0].shape[0] - images
    texts_here = group // devices
    slice_width = width // lanes
    part = message.shape[2] - width

    total = pooled[...]
    for block in arrived[1:]:
        total = total + block[...].astype(F32)[group:]
    image_unit = (
        total * lax.rsqrt(jnp.sum(total * total, axis=1, keepdims=True) + EPS)
    ).astype(BF16)
    text_unit = jnp.concatenate([block[:group] for block in arrived], axis=0)

    own_columns = text_unit[:, :slice_width]
    for lane in range(1, lanes):
        block = text_unit[:, lane * slice_width : (lane + 1) * slice_width]
        own_columns = jnp.where(mp_index == lane, block, own_columns)
    signs = label[...]
    logits = 4.0 * dot(image_unit, text_unit, LAST_LAST) - 2.0
    by_image = -4.0 * signs * jax.nn.sigmoid(-signs * logits)
    text_grad = dot(by_image[:, :group].astype(BF16), image_unit, FIRST_FIRST)
    rows = sum(order[image] * by_image[image : image + 1] for image in range(images))
    image_grad = dot(rows.astype(BF16), own_columns)
    parts = [image_grad[:, which * part : (which + 1) * part] for which in range(texts_here)]
    for position in range(devices):
        first = position * texts_here
        row = [block[position : position + 1] for block in parts]
        both = [text_grad[first : first + texts_here], jnp.concatenate(row, axis=0)]
        target = moved(dp_index, position, digits_of(devices))
        message[target] = jnp.concatenate(both, axis=1).astype(BF16)


def collect(message, image_grad, text_grad):
    texts_here, width = text_grad.shape
    part = message.shape[2] - width
    arrived = message[...].astype(F32)
    text_grad[...] = jnp.sum(arrived[:, :, :width], axis=0)
    for which in range(texts_here):
        columns = slice(which * part, (which + 1) * part)
        for source in range(arrived.shape[0]):
            image_grad[source : source + 1, columns] = arrived[source, which : which + 1, width:]


def call(kernel, out_shape, args, spaces=None, scratch=(), cost=None):
    spaces = spaces or [pltpu.VMEM] * len(args)
    return pl.pallas_call(
        kernel,
        out_shape=out_shape,
        in_specs=[pl.BlockSpec(memory_space=space) for space in spaces],
        out_specs=jax.tree.map(lambda _: pl.BlockSpec(memory_space=pltpu.VMEM), out_shape),
        scratch_shapes=scratch,
        cost_estimate=cost,
        compiler_params=pltpu.CompilerParams(vmem_limit_bytes=32 * 2**20),
    )(*args)


def on_device(patches, counts, dest, w_qkv, w_out, text):
    devices = lax.axis_size("dp")
    lanes = lax.axis_size("mp")
    images = counts.shape[0] // devices
    width = w_qkv.shape[2]
    rows = patches.shape[1]
    texts_here = text.shape[0]
    slice_width = width // lanes
    heads = w_qkv.shape[1] // HD
    dp_digits, mp_digits = digits_of(devices), digits_of(lanes)
    shape = jax.ShapeDtypeStruct

    sources = [counts, dest, patches, w_qkv, w_out, text]
    patches_here, w_qkv_here, w_out_here, text_here, bias, member, spread, chosen = call(
        functools.partial(load, images),
        (
            *(shape(source.shape, source.dtype) for source in sources[2:]),
            shape((rows, rows), F32),
            shape((images, rows), F32),
            shape((heads * images, heads * rows), F32),
            shape((devices, images), F32),
        ),
        [pltpu.with_memory_space_constraint(source, pltpu.HBM) for source in sources],
        [pltpu.HBM] * 6,
        scratch=[
            pltpu.SMEM(counts.shape, jnp.int32),
            pltpu.SMEM(dest.shape, jnp.int32),
            pltpu.SemaphoreType.DMA((6,)),
        ],
        cost=pl.CostEstimate(flops=0, bytes_accessed=6 * w_qkv.size, transcendentals=0),
    )

    offsets = range(lanes)
    pieces = [
        lax.ppermute(patches, "mp", [(moved(i, offset, mp_digits), i) for i in range(lanes)])
        for offset in offsets[1:]
    ]
    texts = [text_here]
    for stride, radix in dp_digits:
        block = jnp.concatenate(texts, axis=0)
        sent = block if len(texts) > 1 else text
        texts = [block] + [fetch(sent, "dp", stride, radix, by) for by in range(1, radix)]

    share, patch_rows = call(
        functools.partial(attend, offsets),
        (shape((images, width), F32), shape((width, rows), BF16)),
        [patches_here, *pieces, bias, member, spread, w_qkv_here, w_out_here],
        scratch=[pltpu.VMEM((width, rows), F32)],
    )
    total = images * devices
    pooled, label, order = call(
        functools.partial(average, lanes, devices, texts_here),
        (
            shape((images, width), F32),
            shape((images, total), F32),
            shape((images, devices, total), F32),
        ),
        [member, chosen, share, patch_rows],
        cost=pl.CostEstimate(flops=10**9, bytes_accessed=0, transcendentals=0),
    )
    others = texts[:0:-1]
    others[:2] = others[1::-1]
    texts = [texts[0], *others]
    message = call(join, shape((devices * texts_here + images, width), BF16), [*texts, share])
    arrived = [message] + [
        lax.ppermute(message, "mp", [(moved(i, offset, mp_digits), i) for i in range(lanes)])
        for offset in offsets[1:]
    ]
    message = call(
        functools.partial(pair, lanes),
        shape((devices, texts_here, width + slice_width // texts_here), BF16),
        [pooled, label, order, arrived[0], *arrived[:0:-1]],
    )
    message = lax.all_to_all(message, "dp", split_axis=0, concat_axis=0, tiled=True)
    return call(
        collect,
        (shape((devices, slice_width), F32), shape((texts_here, width), F32)),
        [message],
    )


def solution(mesh):
    placed = (P("mp", "dp"), P(), P(), P(None, "mp", None), P("mp", None), P(("dp", "mp"), None))
    return jax.shard_map(
        on_device,
        mesh=mesh,
        in_specs=placed,
        out_specs=(P("dp", "mp"), P(("dp", "mp"), None)),
        check_vma=False,
    )
```
